512 devices in a mesh: ctx: 64 (over z, x), kv: 8 (over y, core).
Axes of the slice: x: 4, y: 4, z: 16, core: 2. Of those that a mesh axis runs over, the one named last changes fastest.
Arguments:
- queries: bfloat16 [4096, 4, 64, 128], P(('ctx', 'kv')), may hold values from -60 to 60
- new_keys: bfloat16 [4096, 4, 8, 128], P(('ctx', 'kv')), may hold values from -6 to 50
- new_values: bfloat16 [4096, 4, 8, 128], P(('ctx', 'kv')), may hold values from -6 to 6
- suffix_keys: bfloat16 [4096, 32, 8, 128], P(('ctx', 'kv')), may hold values from -6 to 50
- suffix_values: bfloat16 [4096, 32, 8, 128], P(('ctx', 'kv')), may hold values from -6 to 6
- suffix_length: int32 [4096], P(('ctx', 'kv')), may hold values from 1 to 32, 81920 in all
- row_nodes: int32 [4096, 2], P('ctx'), may hold values from 0 to 63, all different within a row; in each aligned block of 64 rows (0 to 63, 64 to 127, ...) at most 3 rows name the same one
- prefix_keys: bfloat16 [64, 1024, 8, 128], P('ctx', None, 'kv'), may hold values from -6 to 50
- prefix_values: bfloat16 [64, 1024, 8, 128], P('ctx', None, 'kv'), may hold values from -6 to 6
- node_length: int32 [64], P('ctx'), may hold values from 1 to 1024, 49152 in all
Outputs:
- attended: bfloat16 [4096, 4, 64, 128], P(('ctx', 'kv'))
The draws below stay inside these ranges and needn't reach their ends.
Inputs may be any that keep to these rules, and one draw needn't show every extreme that they name: `row_nodes`: each row names 2 different nodes; among the rows of one ctx index (aligned blocks of 64 rows) no node is named by more than 3 rows, and some node is named that often.
All inputs are finite; a program needn't handle non-finite values. No bound on the sum of `suffix_length` or of `node_length` on one device may be relied on, other than what follows from the above.
Results may differ from the reference program's by a relative error of at most 0.012.
Values may be sent and summed in bfloat16 or wider, within the bound.
No kernel may reach another device: no remote copies, remote signals or barrier semaphores. Data moves between devices by JAX's collectives and lax.ppermute only.
A program may use at most 64 MiB of HBM per device.

```python
import math
import jax
import jax.numpy as jnp
import numpy as np
from jax import lax

H = 64
KVH = 8
DH = 128
ROWS_DEV = 64
NODE_LEN = 1024
SUF = 32
DEPTH = 2
STEPS = 4
NODES = 64
ROWS = 4096
CAP = 3


def draw_queries(key, part):
    key = jax.random.fold_in(key, 11)
    subkeys = jax.random.split(key, 1)
    drawn = jax.random.truncated_normal(subkeys[0], -6.0, 6.0, (ROWS, STEPS, H, DH), jnp.float32)
    return drawn.astype(jnp.bfloat16)


def draw_prefix_keys(key, part):
    key = jax.random.fold_in(key, 12)
    first = jax.random.fold_in(key, 0)
    drawn = jax.random.truncated_normal(first, -6.0, 6.0, (NODES, NODE_LEN, KVH, DH), jnp.float32)
    return drawn.astype(jnp.bfloat16)


def draw_suffix_keys(key, part):
    key = jax.random.fold_in(key, 13)
    first = jax.random.fold_in(key, 0)
    drawn = jax.random.truncated_normal(first, -6.0, 6.0, (ROWS, SUF, KVH, DH), jnp.float32)
    return drawn.astype(jnp.bfloat16)


def draw_new_keys(key, part):
    key = jax.random.fold_in(key, 14)
    first = jax.random.fold_in(key, 0)
    drawn = jax.random.truncated_normal(first, -6.0, 6.0, (ROWS, STEPS, KVH, DH), jnp.float32)
    return drawn.astype(jnp.bfloat16)


def steps_of(stream_key, extent, cuts, smallest, largest):
    def one(dim, blocks):
        heights = jax.random.uniform(jax.random.fold_in(jax.random.fold_in(stream_key, 6), dim), (blocks,), jnp.float32, smallest / len(cuts), largest / len(cuts))
        return jnp.repeat(jnp.exp(heights), extent[dim] // blocks).reshape((-1,) + (1,) * (len(extent) - dim - 1))

    level = one(*cuts[0])
    for cut in cuts[1:]:
        level = level * one(*cut)
    return level


def split_up(count, total, bound, skew):
    weights = [(1 << 20) // math.isqrt(standing ** skew) + 1 for standing in range(2, count + 1)]
    rest, counts = total - bound - (count - 1), [1] * (count - 1)
    while rest > 0:
        movable = [i for i in range(count - 1) if counts[i] < bound]
        whole, remaining = sum([weights[i] for i in movable]), rest
        for i in movable:
            more = min(bound - counts[i], max(1, remaining * weights[i] // whole), rest)
            counts[i] = counts[i] + more
            rest = rest - more
    return np.array([bound] + counts)


def ragged_sizes(rng, amount, total, most, skew):
    if amount == 2:
        one = jax.random.randint(rng, (), max(1, total - most), min(most, total - 1) + 1)
        return jnp.stack([one, total - one])
    sizes = jnp.asarray(split_up(amount, total, most, skew), jnp.int32)
    couples = (amount - 1) // 2
    source_of, receiver = sizes[1:1 + 2 * couples:2], sizes[2:2 + 2 * couples:2]
    slack = jnp.minimum(source_of - 1, most - receiver)
    shifted = jax.random.randint(jax.random.fold_in(rng, 1), (couples,), 0, 1 << 20) % (slack + 1)
    sizes = sizes.at[1:1 + 2 * couples:2].set(source_of - shifted).at[2:2 + 2 * couples:2].set(receiver + shifted)
    return sizes[jax.random.permutation(jax.random.fold_in(rng, 2), amount)]


def shared_out(own_key, own, number, rows, amount, top, bound, slope):
    order = jax.random.permutation(own_key, amount)
    crowded, common = load_shares(amount, rows * top, bound, slope, True), load_shares(amount, rows * top, bound, slope, False)
    places = jnp.arange(amount)

    def named(sizes, turn):
        used = int((sizes > 0).sum())
        fixed = max(1, used // 4)
        moved = fixed + (places - fixed + turn * (used - fixed)) % max(1, amount - fixed)
        return jnp.zeros((amount,), jnp.int32).at[order[jnp.where(places < fixed, places, moved)]].set(jnp.asarray(sizes, jnp.int32))

    sizes = jnp.where(number % 4 == 0, named(crowded, number // 4), named(common, number - number // 4 - 1))
    mixed = jax.random.permutation(jax.random.fold_in(own, 3), amount)
    donor, taker = mixed[0:amount // 2 * 2:2], mixed[1:amount // 2 * 2:2]
    room = jnp.minimum(sizes[donor] - 1, bound - sizes[taker]) // 2
    room = jnp.where((donor == order[0]) | (taker == order[0]) | (sizes[taker] == 0), 0, jnp.maximum(room, 0))
    moved = jax.random.randint(jax.random.fold_in(own, 4), (amount // 2,), 0, 1 << 20) % (room + 1)
    sizes = sizes.at[donor].add(-moved).at[taker].add(moved)
    members = jnp.searchsorted(jnp.cumsum(sizes), jnp.arange(rows * top), side="right").astype(jnp.int32)
    grid = members.reshape(top, rows).T
    grid = grid[jax.random.permutation(jax.random.fold_in(own, 1), rows)]
    turn = jax.random.randint(jax.random.fold_in(own, 2), (rows, 1), 0, top)
    return jnp.take_along_axis(grid, (jnp.arange(top)[None, :] + turn) % top, axis=1)


def load_shares(count, total, bound, lean, full):
    loads = [(1 << 20) // math.isqrt(grade ** lean) + 1 for grade in range(1, count + 1)]
    largest = bound if full else min(bound, max(-(-total // count), total * loads[0] // sum(loads)))
    least = 1 if total - largest >= count - 1 else 0
    given, rest = [largest] + [least] * (count - 1), total - largest - least * (count - 1)
    while rest > 0:
        movable = [i for i in range(1, count) if given[i] < largest] or [i for i in range(1, count) if given[i] < bound]
        whole, remaining = sum([loads[i] for i in movable]), rest
        for i in movable:
            extra = min(bound - given[i], max(1, remaining * loads[i] // whole), rest)
            given[i] = given[i] + extra
            rest = rest - extra
    return np.array(given)


def noise(stream_key, dims, scale, reach, shards=(), kind=jnp.bfloat16):
    array = jax.random.normal(stream_key, dims, jnp.float32) * scale
    if len(shards) > 0:
        array = steps_of(stream_key, dims, shards, -0.22, 0.18) * array
    return jnp.clip(array, min=-reach, max=reach).astype(kind)


def setup_inputs(seed: int = 0) -> dict:
    key_of = jax.random.split(jax.random.key(seed), 11)
    queries = draw_queries(jax.random.fold_in(key_of[10], 71), 0)
    new_keys = draw_new_keys(jax.random.fold_in(key_of[10], 71), 0)
    new_values = noise(key_of[2], (ROWS, STEPS, KVH, DH), 1.0, 6.0, ((0, 512),))
    suffix_keys = draw_suffix_keys(jax.random.fold_in(key_of[10], 71), 0)
    suffix_values = noise(key_of[4], (ROWS, SUF, KVH, DH), 1.0, 6.0, ((0, 512),))
    suffix_length = ragged_sizes(key_of[5], ROWS, ROWS * SUF * 5 // 8, SUF, 2).astype(jnp.int32)
    row_nodes_keys = jax.random.split(jax.random.fold_in(key_of[6], 1), ROWS // ROWS_DEV)
    row_nodes_turns = jax.random.permutation(jax.random.fold_in(key_of[6], 3), ROWS // ROWS_DEV)
    row_nodes = jax.vmap(lambda own, number: shared_out(jax.random.fold_in(key_of[6], 2), own, number, ROWS_DEV, NODES, DEPTH, CAP, 2))(row_nodes_keys, row_nodes_turns).reshape((ROWS, DEPTH))
    prefix_keys = draw_prefix_keys(jax.random.fold_in(key_of[10], 71), 0)
    prefix_values = noise(key_of[8], (NODES, NODE_LEN, KVH, DH), 1.0, 6.0, ((0, 64), (2, 8)))
    node_length = ragged_sizes(key_of[9], NODES, NODES * NODE_LEN * 3 // 4, NODE_LEN, 2).astype(jnp.int32)
    return {"queries": queries, "new_keys": new_keys, "new_values": new_values, "suffix_keys": suffix_keys, "suffix_values": suffix_values, "suffix_length": suffix_length, "row_nodes": row_nodes, "prefix_keys": prefix_keys, "prefix_values": prefix_values, "node_length": node_length}


def rounded(values):
    return lax.optimization_barrier(values.astype(jnp.bfloat16)).astype(jnp.float32)


def reference(queries, new_keys, new_values, suffix_keys, suffix_values, suffix_length, row_nodes, prefix_keys, prefix_values, node_length):
    row_block = 8
    group_size = H // KVH
    score_scale = DH ** -0.5

    def one_block(block_index):
        start = (block_index * row_block).astype(jnp.int32)
        query_heads = lax.dynamic_slice_in_dim(queries, start, row_block, 0).astype(jnp.float32)
        query_heads = query_heads.reshape(row_block, STEPS, KVH, group_size, DH)
        nodes = lax.dynamic_slice_in_dim(row_nodes, start, row_block, 0)
        node_keys = jnp.take(prefix_keys, nodes, axis=0).astype(jnp.float32)
        node_values = jnp.take(prefix_values, nodes, axis=0).astype(jnp.float32)
        lengths = jnp.take(node_length, nodes, axis=0)
        scores = jnp.einsum('rsjgd,rnljd->rnsjgl', query_heads, node_keys) * score_scale
        valid = jnp.arange(NODE_LEN)[None, None, :] < lengths[:, :, None]
        scores = jnp.where(valid[:, :, None, None, None, :], scores, -jnp.inf)
        node_max = jnp.max(scores, axis=-1)
        weights = jnp.exp(scores - node_max[..., None])
        node_total = jnp.sum(weights, axis=-1)
        node_output = jnp.einsum('rnsjgl,rnljd->rnsjgd', rounded(weights), node_values) / node_total[..., None]
        node_output = rounded(node_output)

        path_max = jnp.max(node_max, axis=1)
        path_weight = node_total * jnp.exp(node_max - path_max[:, None])
        path_total = jnp.sum(path_weight, axis=1)
        path_output = rounded(jnp.sum(path_weight[..., None] * node_output, axis=1) / path_total[..., None])

        own_keys = lax.dynamic_slice_in_dim(suffix_keys, start, row_block, 0).astype(jnp.float32)
        own_values = lax.dynamic_slice_in_dim(suffix_values, start, row_block, 0).astype(jnp.float32)
        fresh_keys = lax.dynamic_slice_in_dim(new_keys, start, row_block, 0).astype(jnp.float32)
        fresh_values = lax.dynamic_slice_in_dim(new_values, start, row_block, 0).astype(jnp.float32)
        own_length = lax.dynamic_slice_in_dim(suffix_length, start, row_block, 0)
        own_scores = jnp.einsum('rsjgd,rtjd->rsjgt', query_heads, own_keys) * score_scale
        own_valid = jnp.arange(SUF)[None, :] < own_length[:, None]
        own_scores = jnp.where(own_valid[:, None, None, None, :], own_scores, -jnp.inf)
        fresh_scores = jnp.einsum('rsjgd,rtjd->rsjgt', query_heads, fresh_keys) * score_scale
        fresh_valid = jnp.arange(STEPS)[None, :] <= jnp.arange(STEPS)[:, None]
        fresh_scores = jnp.where(fresh_valid[None, :, None, None, :], fresh_scores, -jnp.inf)
        suffix_max = jnp.maximum(jnp.max(own_scores, axis=-1), jnp.max(fresh_scores, axis=-1))
        own_weights = jnp.exp(own_scores - suffix_max[..., None])
        fresh_weights = jnp.exp(fresh_scores - suffix_max[..., None])
        suffix_total = jnp.sum(own_weights, axis=-1) + jnp.sum(fresh_weights, axis=-1)
        suffix_sum = jnp.einsum('rsjgt,rtjd->rsjgd', rounded(own_weights), own_values)
        suffix_sum = suffix_sum + jnp.einsum('rsjgt,rtjd->rsjgd', rounded(fresh_weights), fresh_values)

        top_score = jnp.maximum(path_max, suffix_max)
        weight_prefix = path_total * jnp.exp(path_max - top_score)
        weight_suffix = jnp.exp(suffix_max - top_score)
        numerator = weight_prefix[..., None] * path_output + weight_suffix[..., None] * suffix_sum
        denominator = weight_prefix + weight_suffix * suffix_total
        result = numerator / denominator[..., None]
        return result.reshape(row_block, STEPS, H, DH).astype(jnp.bfloat16)

    blocks = lax.map(one_block, jnp.arange(ROWS // row_block, dtype=jnp.int32))
    return blocks.reshape(ROWS, STEPS, H, DH)
```

```python
import functools
import math

import jax
import jax.numpy as jnp
from jax import lax
from jax.experimental import pallas as pl
from jax.experimental.pallas import tpu as pltpu
from jax.sharding import Mesh
from jax.sharding import PartitionSpec as P

NZ, NX, NY, NC = 16, 4, 4, 2
NKV = NY * NC
CAP = 3
F32 = jnp.float32
BF16 = jnp.bfloat16
VMEM_LIMIT = 48 * 1024 * 1024
VM = pl.BlockSpec(memory_space=pltpu.VMEM)


def params():
    return pltpu.CompilerParams(vmem_limit_bytes=VMEM_LIMIT)


def split3(x):
    hi = x.astype(BF16).astype(F32)
    rest = x - hi
    mid = rest.astype(BF16).astype(F32)
    return [hi, mid, rest - mid]


def lane_stats(values, rows):
    lane = lax.broadcasted_iota(jnp.int32, (rows, 128), 1)
    out = jnp.zeros((rows, 128), F32)
    for i, v in enumerate(values):
        out = jnp.where(lane == i, v, out)
    return out


def pad_rows(x, rows):
    if x.shape[0] == rows:
        return x
    return jnp.concatenate([x, jnp.zeros((rows - x.shape[0], x.shape[1]), x.dtype)], axis=0)


def suffix_kernel(scale, steps, len_ref, q_ref, k_ref, nk_ref, v_ref, nv_ref, sum_ref, stat_ref):
    row = pl.program_id(0)
    length = len_ref[row]
    q = q_ref[0]
    heads = q.shape[0] // steps
    kvh = nk_ref.shape[1] // steps
    group = heads // kvh

    def scores(keys):
        return lax.dot_general(q, keys, (((1,), (1,)), ((), ())), preferred_element_type=F32) * scale

    def masks(cols):
        qi = lax.broadcasted_iota(jnp.int32, (q.shape[0], cols), 0)
        ci = lax.broadcasted_iota(jnp.int32, (q.shape[0], cols), 1)
        same = ((qi % heads) // group) == (ci % kvh)
        return same, ci // kvh, qi // heads

    same, slot, _ = masks(k_ref.shape[1])
    own = jnp.where(same & (slot < length), scores(k_ref[0]), -jnp.inf)
    same, slot, step = masks(nk_ref.shape[1])
    fresh = jnp.where(same & (slot <= step), scores(nk_ref[0]), -jnp.inf)
    top = jnp.maximum(jnp.max(own, axis=1, keepdims=True), jnp.max(fresh, axis=1, keepdims=True))
    own_w = jnp.exp(own - top)
    fresh_w = jnp.exp(fresh - top)
    total = jnp.sum(own_w, axis=1, keepdims=True) + jnp.sum(fresh_w, axis=1, keepdims=True)
    acc = jnp.dot(own_w.astype(BF16), v_ref[0], preferred_element_type=F32)
    acc = acc + jnp.dot(fresh_w.astype(BF16), nv_ref[0], preferred_element_type=F32)
    sum_ref[0] = acc
    both = lane_stats([top, total], q.shape[0])
    for b in range(0, q.shape[0], 128):
        columns = both[b : b + 128]
        stat_ref[0, :, b : b + 128] = pad_rows(columns, 128).T[:8, : columns.shape[0]]


def suffix_part(queries, new_keys, new_values, suffix_keys, suffix_values, suffix_length):
    rows, steps, heads, dim = queries.shape
    slots, kvh = suffix_keys.shape[1:3]
    qn, kn, fn = steps * heads, slots * kvh, steps * kvh
    block = lambda n: pl.BlockSpec((1, n, dim), lambda i, s: (i, 0, 0))
    ssum, sstat = pl.pallas_call(
        functools.partial(suffix_kernel, dim ** (-0.5), steps),
        grid_spec=pltpu.PrefetchScalarGridSpec(
            num_scalar_prefetch=1,
            grid=(rows,),
            in_specs=[block(qn), block(kn), block(fn), block(kn), block(fn)],
            out_specs=[block(qn), pl.BlockSpec((1, 8, qn), lambda i, s: (i, 0, 0))],
        ),
        out_shape=[
            jax.ShapeDtypeStruct((rows, qn, dim), F32),
            jax.ShapeDtypeStruct((rows, 8, qn), F32),
        ],
        compiler_params=params(),
        cost_estimate=pl.CostEstimate(
            flops=4 * rows * qn * kn * dim, bytes_accessed=4 << 20, transcendentals=rows * qn * kn
        ),
        name="suffix",
    )(
        suffix_length,
        queries.reshape(rows, qn, dim),
        suffix_keys.reshape(rows, kn, dim),
        new_keys.reshape(rows, fn, dim),
        suffix_values.reshape(rows, kn, dim),
        new_values.reshape(rows, fn, dim),
    )
    group = heads // kvh
    stat = sstat[:, :2].reshape(rows, 2, steps, kvh, group).transpose(1, 3, 0, 2, 4)
    stat = stat.reshape(2, kvh, rows, steps * group)
    return ssum, jnp.pad(stat, ((0, 0), (0, 0), (0, 0), (0, 128 - steps * group)))


def pack_kernel(table_ref, q_ref, out_ref):
    rows = q_ref.shape[0]

    def one(j, carry):
        entry = jnp.maximum(table_ref[j], 0)
        out_ref[j] = q_ref[lax.rem(entry, rows)]
        return carry

    lax.fori_loop(0, out_ref.shape[0], one, 0, unroll=8)


def pack_part(table, grouped):
    rows, per_row, dim = grouped.shape
    return pl.pallas_call(
        pack_kernel,
        grid_spec=pltpu.PrefetchScalarGridSpec(
            num_scalar_prefetch=1, grid=(), in_specs=[VM], out_specs=VM
        ),
        out_shape=jax.ShapeDtypeStruct((table.shape[0], per_row, dim), BF16),
        compiler_params=params(),
        cost_estimate=pl.CostEstimate(flops=1 << 16, bytes_accessed=2 << 20, transcendentals=0),
        name="pack",
    )(table, grouped)


def node_kernel(scale, count, *refs):
    q_refs, kv_refs, out_ref = refs[:count], refs[count:-1], refs[-1]
    stats = []
    for i in range(count):
        q = q_refs[i][...]
        each = q.shape[1] * q.shape[2]
        m_all = NX * each
        q = q.reshape(m_all, q.shape[3])
        slots = (kv_refs[i].shape[0] - 16) // 2
        keys, values, tail = kv_refs[i][:slots], kv_refs[i][slots : 2 * slots], kv_refs[i][2 * slots :]
        length = tail[:8].astype(F32)
        length = length[0:1, :] * 32.0 + length[1:2, :]
        length = jnp.concatenate([length] * (slots // 128), axis=1)
        s = lax.dot_general(q, keys, (((1,), (1,)), ((), ())), preferred_element_type=F32)
        col = lax.broadcasted_iota(jnp.int32, (1, slots), 1).astype(F32)
        s = jnp.where(col < length, s, -jnp.inf)
        top = jnp.max(s, axis=1, keepdims=True)
        w = jnp.exp2((s - top) * (scale * math.log2(math.e)))
        total = jnp.sum(w, axis=1, keepdims=True)
        o = jnp.dot(w.astype(BF16), values, preferred_element_type=F32) * (1.0 / total)
        o = o.astype(BF16).reshape(NX, each, o.shape[1])
        for x in range(NX):
            out_ref[x, i * each : (i + 1) * each] = o[x]
        stats += split3(top * scale) + split3(total)
    packed = lane_stats(stats, m_all)
    for x in range(NX):
        block = pad_rows(packed[x * each : (x + 1) * each], 128)
        out_ref[x, count * each :] = block.T[: out_ref.shape[1] - count * each].astype(BF16)


def node_part(q_slots, offsets, kvs):
    count = len(offsets)
    per_row, dim = q_slots.shape[2:]
    each = CAP * per_row
    work = NX * each * 1024 * count
    q_block = lambda off: pl.BlockSpec((NX, CAP, per_row, dim), lambda i: (0, off, 0, 0))
    return pl.pallas_call(
        functools.partial(node_kernel, dim ** (-0.5), count),
        grid=(1,),
        in_specs=[q_block(o) for o in offsets] + [VM] * len(kvs),
        out_specs=pl.BlockSpec((NX, count * each + 16, dim), lambda i: (0, 0, 0)),
        out_shape=jax.ShapeDtypeStruct((NX, count * each + 16, dim), BF16),
        compiler_params=params(),
        cost_estimate=pl.CostEstimate(flops=4 * work * dim, bytes_accessed=count << 20, transcendentals=work),
        name="node",
    )(*[q_slots] * count, *kvs)


def merge_kernel(groups, rows, per_row, table_ref, *refs):
    arrived = refs[: len(groups)]
    out_ref, e_out, e_max, e_total = refs[len(groups) :]
    each = CAP * per_row
    for ref, steps in zip(arrived, groups):
        base = 0
        for offsets in steps:
            count = len(offsets)
            for x in range(NX):
                tile = ref[x, base + count * each : base + count * each + 16].astype(F32)
                for i, off in enumerate(offsets):
                    top = tile[6 * i : 6 * i + 1] + tile[6 * i + 1 : 6 * i + 2] + tile[6 * i + 2 : 6 * i + 3]
                    total = tile[6 * i + 3 : 6 * i + 4] + tile[6 * i + 4 : 6 * i + 5] + tile[6 * i + 5 : 6 * i + 6]
                    for k in range(CAP):
                        entry = table_ref[(x * NZ + off) * CAP + k]
                        entry = jnp.where(entry < 0, 2 * rows, entry)
                        start = base + i * each + k * per_row
                        e_out[entry] = ref[x, start : start + per_row]
                        if k:
                            top_k = pltpu.roll(top, 128 - k * per_row, 1)
                            total_k = pltpu.roll(total, 128 - k * per_row, 1)
                        else:
                            top_k, total_k = top, total
                        e_max[pl.ds(entry, 1), :] = top_k
                        e_total[pl.ds(entry, 1), :] = total_k
            base += count * each + 16
    m0, m1 = e_max[:rows], e_max[rows : 2 * rows]
    top = jnp.maximum(m0, m1)
    w0 = e_total[:rows] * jnp.exp(m0 - top)
    w1 = e_total[rows : 2 * rows] * jnp.exp(m1 - top)
    total = w0 + w1
    f0 = pad_rows(w0 / total, 128).T
    f1 = pad_rows(w1 / total, 128).T
    rows_here = rows // NKV
    pieces = split3(top) + split3(total)
    tail = rows_here * per_row
    for y in range(NKV):
        for r in range(rows_here):
            row = y * rows_here + r
            o = f0[:per_row, row : row + 1] * e_out[row].astype(F32)
            o = o + f1[:per_row, row : row + 1] * e_out[rows + row].astype(F32)
            out_ref[y, r * per_row : (r + 1) * per_row] = o.astype(BF16)
        part = [p[y * rows_here : (y + 1) * rows_here] for p in pieces]
        part = pad_rows(jnp.concatenate(part, axis=0), out_ref.shape[1] - tail)
        out_ref[y, tail:] = part.astype(BF16)


def merge_part(table, arrived, groups, rows, per_row):
    dim = arrived[0].shape[2]
    rows_here = rows // NKV
    stat_rows = -(-6 * rows_here // 16) * 16
    shape = (NKV, rows_here * per_row + stat_rows, dim)
    return pl.pallas_call(
        functools.partial(merge_kernel, groups, rows, per_row),
        grid_spec=pltpu.PrefetchScalarGridSpec(
            num_scalar_prefetch=1,
            grid=(),
            in_specs=[VM] * len(arrived),
            out_specs=VM,
            scratch_shapes=[
                pltpu.VMEM((2 * rows + 1, per_row, dim), BF16),
                pltpu.VMEM((2 * rows + 8, 128), F32),
                pltpu.VMEM((2 * rows + 8, 128), F32),
            ],
        ),
        out_shape=jax.ShapeDtypeStruct(shape, BF16),
        compiler_params=params(),
        cost_estimate=pl.CostEstimate(flops=1 << 22, bytes_accessed=4 << 20, transcendentals=1 << 16),
        name="merge",
    )(table, *arrived)


def final_kernel(rows, steps, arrived_ref, ssum_ref, sstat_ref, out_ref, res_ref):
    group = ssum_ref.shape[2]
    per_row = steps * group
    here = rows * per_row
    w_prefix, w_suffix = [], []
    for j in range(NKV):
        tile = arrived_ref[j, here:].astype(F32)
        part = [tile[i * rows : (i + 1) * rows] for i in range(6)]
        p_max, p_total = part[0] + part[1] + part[2], part[3] + part[4] + part[5]
        s_max, s_total = sstat_ref[0, j], sstat_ref[1, j]
        top = jnp.maximum(p_max, s_max)
        wp = p_total * jnp.exp(p_max - top)
        ws = jnp.exp(s_max - top)
        inverse = 1.0 / (wp + ws * s_total)
        w_prefix.append(wp * inverse)
        w_suffix.append(ws * inverse)
    w_prefix = pad_rows(jnp.concatenate(w_prefix, axis=0), 128).T
    w_suffix = pad_rows(jnp.concatenate(w_suffix, axis=0), 128).T
    for j in range(NKV):
        for r in range(rows):
            at = j * rows + r
            o = arrived_ref[j, r * per_row : (r + 1) * per_row].astype(F32)
            own = ssum_ref[r * steps : (r + 1) * steps, j].reshape(per_row, o.shape[1])
            mixed = w_prefix[:per_row, at : at + 1] * o + w_suffix[:per_row, at : at + 1] * own
            res_ref[r * steps : (r + 1) * steps, j] = mixed.reshape(steps, group, o.shape[1])
    out_ref[...] = res_ref[...].reshape(out_ref.shape).astype(BF16)


def final_part(arrived, ssum, sstat, rows, steps, heads, dim):
    shape = (rows * steps, NKV, heads // NKV, dim)
    out = pl.pallas_call(
        functools.partial(final_kernel, rows, steps),
        in_specs=[VM] * 3,
        out_specs=VM,
        out_shape=jax.ShapeDtypeStruct((rows * steps * heads, dim), BF16),
        scratch_shapes=[pltpu.VMEM(shape, F32)],
        compiler_params=params(),
        cost_estimate=pl.CostEstimate(flops=1 << 22, bytes_accessed=4 << 20, transcendentals=1 << 16),
        name="final",
    )(arrived, ssum.reshape(shape), sstat)
    return out.reshape(rows, steps, heads, dim)


def entry_table(row_nodes, zi):
    rows, depth = row_nodes.shape
    node = row_nodes.T.reshape(rows * depth)
    entry = jnp.arange(rows * depth, dtype=jnp.int32)
    earlier = (node[:, None] == node[None, :]) & (entry[None, :] < entry[:, None])
    rank = jnp.sum(earlier.astype(jnp.int32), axis=1)
    offset = jnp.mod(node // NX - zi, NZ)
    place = (jnp.mod(node, NX) * NZ + offset) * CAP + rank
    hit = place[:, None] == jnp.arange(NX * NZ * CAP, dtype=jnp.int32)[None, :]
    return jnp.sum(jnp.where(hit, entry[:, None] + 1, 0), axis=0) - 1


def per_device(
    queries, new_keys, new_values, suffix_keys, suffix_values, suffix_length,
    row_nodes, prefix_keys, prefix_values, node_length,
):
    rows_dev, depth = row_nodes.shape
    rows_here, steps, heads, dim = queries.shape
    group = heads // NKV
    per_row = steps * group
    zi = lax.axis_index("z")
    half = NZ // 2

    slots = prefix_keys.shape[1]
    length = node_length[0]
    digits = jnp.stack([length // 32, length % 32]).astype(BF16)
    tail = jnp.broadcast_to(jnp.pad(digits, (0, 14))[:, None], (16, dim))
    own = jnp.concatenate([prefix_keys.reshape(slots, dim), prefix_values.reshape(slots, dim), tail])
    up = [(i, (i + 1) % NZ) for i in range(NZ)]
    down = [(i, (i - 1) % NZ) for i in range(NZ)]

    tie = lax.optimization_barrier
    by_head = queries.reshape(rows_here * steps, NKV, group, dim).transpose(1, 0, 2, 3)
    by_head, own = tie((by_head, own))
    grouped = lax.all_to_all(by_head, ("y", "core"), split_axis=0, concat_axis=0, tiled=True)
    grouped = grouped.reshape(rows_dev, per_row, dim)
    table = entry_table(row_nodes, zi)
    ssum, sstat = suffix_part(queries, new_keys, new_values, suffix_keys, suffix_values, suffix_length)

    plan = [[0]] + [[NZ - s, s] for s in range(1, half)] + [[half]]
    cuts = [range(0, 4), range(4, half - 1), range(half - 1, half + 1)]
    groups = [[plan[s] for s in cut] for cut in cuts]

    def send_back(blocks):
        return lax.all_to_all(jnp.concatenate(blocks, axis=1), "x", split_axis=0, concat_axis=0, tiled=True)

    due = {2: [], 4: [], 5: [0, 1, 2], 6: [3, 4], 7: [5, 6]}
    arrived = [[own]]
    sent = []
    going_up = going_down = own
    for s in range(1, half):
        going_up, going_down = lax.ppermute(going_up, "z", up), lax.ppermute(going_down, "z", down)
        if s == 2:
            going_up, grouped = tie((going_up, grouped))
            packed = pack_part(table, grouped).reshape(NX, NZ * CAP, per_row, dim)
            q_slots = lax.all_to_all(packed, "x", split_axis=0, concat_axis=0, tiled=True)
        elif s == 4:
            going_up, q_slots = tie((going_up, q_slots))
        if due.get(s):
            fresh = [node_part(q_slots, plan[t], arrived[t]) for t in due[s]]
            going_up, fresh = tie((going_up, fresh))
            sent += fresh
        arrived.append([going_up, going_down])
    farthest = lax.ppermute(going_up, "z", up)
    sent.append(node_part(q_slots, plan[half - 1], arrived[half - 1]))
    sent.append(node_part(q_slots, plan[half], [farthest]))
    back = [send_back([sent[s] for s in cut]) for cut in cuts]
    merged = merge_part(table, back, groups, rows_dev, per_row)
    home = lax.all_to_all(merged, ("y", "core"), split_axis=0, concat_axis=0, tiled=True)
    return final_part(home, ssum, sstat, rows_here, steps, heads, dim)


def solution(mesh):
    fine = Mesh(mesh.devices.reshape(NZ, NX, NY, NC), ("z", "x", "y", "core"))
    ctx, kv = ("z", "x"), ("y", "core")
    everything = ctx + kv
    return jax.shard_map(
        per_device,
        mesh=fine,
        in_specs=(
            P(everything), P(everything), P(everything), P(everything), P(everything), P(everything),
            P(ctx, None),
            P(ctx, None, kv, None),
            P(ctx, None, kv, None),
            P(ctx),
        ),
        out_specs=P(everything),
        check_vma=False,
    )
```

```python
import functools
import math

import jax
import jax.numpy as jnp
from jax import lax
from jax.experimental import pallas as pl
from jax.experimental.pallas import tpu as pltpu
from jax.sharding import Mesh
from jax.sharding import PartitionSpec as P

NZ, NX, NY, NC = 16, 4, 4, 2
NKV = NY * NC
CAP = 3
CALLS = [[0, 1], [2, 3, 4], [5], [6], [7]]
DUE = [4, 5, 6, 7, 8]
CUTS = [[0, 1, 2], [3, 4]]
F32 = jnp.float32
BF16 = jnp.bfloat16
VMEM_LIMIT = 20 * 1024 * 1024
VM = pl.BlockSpec(memory_space=pltpu.VMEM)


SMALL = pl.CostEstimate(flops=1 << 10, bytes_accessed=1 << 10, transcendentals=0)


def params():
    return pltpu.CompilerParams(vmem_limit_bytes=VMEM_LIMIT)


def split3(x):
    hi = x.astype(BF16).astype(F32)
    rest = x - hi
    mid = rest.astype(BF16).astype(F32)
    return [hi, mid, rest - mid]


def lane_stats(values, rows):
    lane = lax.broadcasted_iota(jnp.int32, (rows, 128), 1)
    out = jnp.zeros((rows, 128), F32)
    for i, v in enumerate(values):
        out = jnp.where(lane == i, v, out)
    return out


def pad_rows(x, rows):
    if x.shape[0] == rows:
        return x
    return jnp.concatenate([x, jnp.zeros((rows - x.shape[0], x.shape[1]), x.dtype)], axis=0)


def suffix_kernel(scale, steps, len_ref, q_ref, k_ref, nk_ref, v_ref, nv_ref, sum_ref, stat_ref):
    row = pl.program_id(0)
    length = len_ref[row]
    q = q_ref[0]
    heads = q.shape[0] // steps
    kvh = nk_ref.shape[1] // steps
    group = heads // kvh

    def scores(keys):
        return lax.dot_general(q, keys, (((1,), (1,)), ((), ())), preferred_element_type=F32) * scale

    def masks(cols):
        qi = lax.broadcasted_iota(jnp.int32, (q.shape[0], cols), 0)
        ci = lax.broadcasted_iota(jnp.int32, (q.shape[0], cols), 1)
        same = ((qi % heads) // group) == (ci % kvh)
        return same, ci // kvh, qi // heads

    same, slot, _ = masks(k_ref.shape[1])
    own = jnp.where(same & (slot < length), scores(k_ref[0]), -jnp.inf)
    same, slot, step = masks(nk_ref.shape[1])
    fresh = jnp.where(same & (slot <= step), scores(nk_ref[0]), -jnp.inf)
    top = jnp.maximum(jnp.max(own, axis=1, keepdims=True), jnp.max(fresh, axis=1, keepdims=True))
    own_w = jnp.exp(own - top)
    fresh_w = jnp.exp(fresh - top)
    total = jnp.sum(own_w, axis=1, keepdims=True) + jnp.sum(fresh_w, axis=1, keepdims=True)
    acc = jnp.dot(own_w.astype(BF16), v_ref[0], preferred_element_type=F32)
    acc = acc + jnp.dot(fresh_w.astype(BF16), nv_ref[0], preferred_element_type=F32)
    sum_ref[0] = acc
    both = lane_stats([top, total], q.shape[0])
    for b in range(0, q.shape[0], 128):
        columns = both[b : b + 128]
        stat_ref[0, :, b : b + 128] = pad_rows(columns, 128).T[:8, : columns.shape[0]]


def suffix_part(queries, new_keys, new_values, suffix_keys, suffix_values, suffix_length):
    rows, steps, heads, dim = queries.shape
    slots, kvh = suffix_keys.shape[1:3]
    qn, kn, fn = steps * heads, slots * kvh, steps * kvh
    block = lambda n: pl.BlockSpec((1, n, dim), lambda i, s: (i, 0, 0))
    ssum, sstat = pl.pallas_call(
        functools.partial(suffix_kernel, dim ** (-0.5), steps),
        grid_spec=pltpu.PrefetchScalarGridSpec(
            num_scalar_prefetch=1,
            grid=(rows,),
            in_specs=[block(qn), block(kn), block(fn), block(kn), block(fn)],
            out_specs=[block(qn), pl.BlockSpec((1, 8, qn), lambda i, s: (i, 0, 0))],
        ),
        out_shape=[
            jax.ShapeDtypeStruct((rows, qn, dim), F32),
            jax.ShapeDtypeStruct((rows, 8, qn), F32),
        ],
        compiler_params=params(),
        cost_estimate=pl.CostEstimate(
            flops=4 * rows * qn * kn * dim, bytes_accessed=4 << 20, transcendentals=rows * qn * kn
        ),
        name="suffix",
    )(
        suffix_length,
        queries.reshape(rows, qn, dim),
        suffix_keys.reshape(rows, kn, dim),
        new_keys.reshape(rows, fn, dim),
        suffix_values.reshape(rows, kn, dim),
        new_values.reshape(rows, fn, dim),
    )
    group = heads // kvh
    stat = sstat[:, :2].reshape(rows, 2, steps, kvh, group).transpose(1, 3, 0, 2, 4)
    stat = stat.reshape(2, kvh, rows, steps * group)
    return ssum, jnp.pad(stat, ((0, 0), (0, 0), (0, 0), (0, 128 - steps * group)))


def pack_kernel(table_ref, q_ref, out_ref):
    rows = q_ref.shape[0]

    def one(j, carry):
        entry = jnp.maximum(table_ref[j], 0)
        out_ref[j] = q_ref[lax.rem(entry, rows)]
        return carry

    lax.fori_loop(0, out_ref.shape[0], one, 0, unroll=8)


def pack_part(table, grouped):
    rows, per_row, dim = grouped.shape
    return pl.pallas_call(
        pack_kernel,
        grid_spec=pltpu.PrefetchScalarGridSpec(
            num_scalar_prefetch=1, grid=(), in_specs=[VM], out_specs=VM
        ),
        out_shape=jax.ShapeDtypeStruct((table.shape[0], per_row, dim), BF16),
        compiler_params=params(),
        cost_estimate=SMALL,
        name="pack",
    )(table, grouped)


def node_kernel(scale, count, *refs):
    q_refs, kv_refs, out_ref = refs[:count], refs[count:-1], refs[-1]
    stats = []
    for i in range(count):
        q = q_refs[i][...]
        each = q.shape[1] * q.shape[2]
        m_all = NX * each
        q = q.reshape(m_all, q.shape[3])
        slots = (kv_refs[i].shape[0] - 16) // 2
        keys, values, tail = kv_refs[i][:slots], kv_refs[i][slots : 2 * slots], kv_refs[i][2 * slots :]
        length = tail[:8].astype(F32)
        length = length[0:1, :] * 32.0 + length[1:2, :]
        length = jnp.concatenate([length] * (slots // 128), axis=1)
        s = lax.dot_general(q, keys, (((1,), (1,)), ((), ())), preferred_element_type=F32)
        col = lax.broadcasted_iota(jnp.int32, (1, slots), 1).astype(F32)
        s = jnp.where(col < length, s, -jnp.inf)
        top = jnp.max(s, axis=1, keepdims=True)
        w = jnp.exp2((s - top) * (scale * math.log2(math.e)))
        total = jnp.sum(w, axis=1, keepdims=True)
        o = jnp.dot(w.astype(BF16), values, preferred_element_type=F32) * (1.0 / total)
        o = o.astype(BF16).reshape(NX, each, o.shape[1])
        for x in range(NX):
            out_ref[x, i * each : (i + 1) * each] = o[x]
        stats += split3(top * scale) + split3(total)
    packed = lane_stats(stats, m_all)
    for x in range(NX):
        block = pad_rows(packed[x * each : (x + 1) * each], 128)
        out_ref[x, count * each :] = block.T[: out_ref.shape[1] - count * each].astype(BF16)


def stat_rows(count):
    return -(-6 * count // 16) * 16


def node_part(q_slots, places, kvs):
    count = len(places)
    per_row, dim = q_slots.shape[2:]
    each = CAP * per_row
    work = NX * each * 1024 * count
    shape = (NX, count * each + stat_rows(count), dim)
    q_block = lambda off: pl.BlockSpec((NX, CAP, per_row, dim), lambda i: (0, off, 0, 0))
    return pl.pallas_call(
        functools.partial(node_kernel, dim ** (-0.5), count),
        grid=(1,),
        in_specs=[q_block(p) for p in places] + [VM] * len(kvs),
        out_specs=pl.BlockSpec(shape, lambda i: (0, 0, 0)),
        out_shape=jax.ShapeDtypeStruct(shape, BF16),
        compiler_params=params(),
        cost_estimate=SMALL,
        name="node",
    )(*[q_slots] * count, *kvs)


def merge_kernel(groups, rows, per_row, table_ref, *refs):
    arrived = refs[: len(groups)]
    out_ref, e_out, e_max, e_total = refs[-4:]
    each = CAP * per_row
    for ref, steps in zip(arrived, groups):
        base = 0
        for offsets in steps:
            count = len(offsets)
            for x in range(NX):
                tile = ref[x, base + count * each : base + count * each + stat_rows(count)].astype(F32)
                for i, off in enumerate(offsets):
                    top = tile[6 * i : 6 * i + 1] + tile[6 * i + 1 : 6 * i + 2] + tile[6 * i + 2 : 6 * i + 3]
                    total = tile[6 * i + 3 : 6 * i + 4] + tile[6 * i + 4 : 6 * i + 5] + tile[6 * i + 5 : 6 * i + 6]
                    for k in range(CAP):
                        entry = table_ref[(x * NZ + off) * CAP + k]
                        entry = jnp.where(entry < 0, 2 * rows, entry)
                        start = base + i * each + k * per_row
                        e_out[entry] = ref[x, start : start + per_row]
                        if k:
                            top_k = pltpu.roll(top, 128 - k * per_row, 1)
                            total_k = pltpu.roll(total, 128 - k * per_row, 1)
                        else:
                            top_k, total_k = top, total
                        e_max[pl.ds(entry, 1), :] = top_k
                        e_total[pl.ds(entry, 1), :] = total_k
            base += count * each + stat_rows(count)
    m0, m1 = e_max[:rows], e_max[rows : 2 * rows]
    top = jnp.maximum(m0, m1)
    w0 = e_total[:rows] * jnp.exp(m0 - top)
    w1 = e_total[rows : 2 * rows] * jnp.exp(m1 - top)
    total = w0 + w1
    f0 = pad_rows(w0 / total, 128).T
    f1 = pad_rows(w1 / total, 128).T
    rows_here = rows // NKV
    pieces = split3(top) + split3(total)
    tail = rows_here * per_row
    for y in range(NKV):
        for r in range(rows_here):
            row = y * rows_here + r
            o = f0[:per_row, row : row + 1] * e_out[row].astype(F32)
            o = o + f1[:per_row, row : row + 1] * e_out[rows + row].astype(F32)
            out_ref[y, r * per_row : (r + 1) * per_row] = o.astype(BF16)
        part = [p[y * rows_here : (y + 1) * rows_here] for p in pieces]
        part = pad_rows(jnp.concatenate(part, axis=0), out_ref.shape[1] - tail)
        out_ref[y, tail:] = part.astype(BF16)


def merge_part(table, arrived, groups, rows, per_row):
    dim = arrived[0].shape[2]
    rows_here = rows // NKV
    shape = (NKV, rows_here * per_row + stat_rows(rows_here), dim)
    return pl.pallas_call(
        functools.partial(merge_kernel, groups, rows, per_row),
        grid_spec=pltpu.PrefetchScalarGridSpec(
            num_scalar_prefetch=1,
            grid=(),
            in_specs=[VM] * len(arrived),
            out_specs=VM,
            scratch_shapes=[
                pltpu.VMEM((2 * rows + 1, per_row, dim), BF16),
                pltpu.VMEM((2 * rows + 8, 128), F32),
                pltpu.VMEM((2 * rows + 8, 128), F32),
            ],
        ),
        out_shape=jax.ShapeDtypeStruct(shape, BF16),
        compiler_params=params(),
        cost_estimate=pl.CostEstimate(flops=1 << 22, bytes_accessed=4 << 20, transcendentals=1 << 16),
        name="merge",
    )(table, *arrived)


def final_kernel(rows, steps, arrived_ref, ssum_ref, sstat_ref, out_ref, res_ref):
    group = ssum_ref.shape[2]
    per_row = steps * group
    here = rows * per_row
    w_prefix, w_suffix = [], []
    for j in range(NKV):
        tile = arrived_ref[j, here:].astype(F32)
        part = [tile[i * rows : (i + 1) * rows] for i in range(6)]
        p_max, p_total = part[0] + part[1] + part[2], part[3] + part[4] + part[5]
        s_max, s_total = sstat_ref[0, j], sstat_ref[1, j]
        top = jnp.maximum(p_max, s_max)
        wp = p_total * jnp.exp(p_max - top)
        ws = jnp.exp(s_max - top)
        inverse = 1.0 / (wp + ws * s_total)
        w_prefix.append(wp * inverse)
        w_suffix.append(ws * inverse)
    w_prefix = pad_rows(jnp.concatenate(w_prefix, axis=0), 128).T
    w_suffix = pad_rows(jnp.concatenate(w_suffix, axis=0), 128).T
    for j in range(NKV):
        for r in range(rows):
            at = j * rows + r
            o = arrived_ref[j, r * per_row : (r + 1) * per_row].astype(F32)
            own = ssum_ref[r * steps : (r + 1) * steps, j].reshape(per_row, o.shape[1])
            mixed = w_prefix[:per_row, at : at + 1] * o + w_suffix[:per_row, at : at + 1] * own
            res_ref[r * steps : (r + 1) * steps, j] = mixed.reshape(steps, group, o.shape[1])
    out_ref[...] = res_ref[...].reshape(out_ref.shape).astype(BF16)


def final_part(arrived, ssum, sstat, rows, steps, heads, dim):
    shape = (rows * steps, NKV, heads // NKV, dim)
    out = pl.pallas_call(
        functools.partial(final_kernel, rows, steps),
        in_specs=[VM] * 3,
        out_specs=VM,
        out_shape=jax.ShapeDtypeStruct((rows * steps * heads, dim), BF16),
        scratch_shapes=[pltpu.VMEM(shape, F32)],
        compiler_params=params(),
        cost_estimate=pl.CostEstimate(flops=1 << 22, bytes_accessed=4 << 20, transcendentals=1 << 16),
        name="final",
    )(arrived, ssum.reshape(shape), sstat)
    return out.reshape(rows, steps, heads, dim)


def entry_table(row_nodes, zi):
    rows, depth = row_nodes.shape
    node = row_nodes.T.reshape(rows * depth)
    entry = jnp.arange(rows * depth, dtype=jnp.int32)
    earlier = (node[:, None] == node[None, :]) & (entry[None, :] < entry[:, None])
    rank = jnp.sum(earlier.astype(jnp.int32), axis=1)
    offset = jnp.mod(node // NX - zi, NZ)
    place = (jnp.mod(node, NX) * NZ + offset) * CAP + rank
    hit = place[:, None] == jnp.arange(NX * NZ * CAP, dtype=jnp.int32)[None, :]
    return jnp.sum(jnp.where(hit, entry[:, None] + 1, 0), axis=0) - 1


def per_device(
    queries, new_keys, new_values, suffix_keys, suffix_values, suffix_length,
    row_nodes, prefix_keys, prefix_values, node_length,
):
    rows_dev, depth = row_nodes.shape
    rows_here, steps, heads, dim = queries.shape
    group = heads // NKV
    per_row = steps * group
    zi = lax.axis_index("z")
    slots = prefix_keys.shape[1]
    length = node_length[0]
    digits = jnp.stack([length // 32, length % 32]).astype(BF16)
    tail = jnp.broadcast_to(jnp.pad(digits, (0, 14))[:, None], (16, dim))
    own = jnp.concatenate([prefix_keys.reshape(slots, dim), prefix_values.reshape(slots, dim), tail])
    up = [(i, (i + 1) % NZ) for i in range(NZ)]
    down = [(i, (i - 1) % NZ) for i in range(NZ)]

    tie = lax.optimization_barrier
    by_head = queries.reshape(rows_here * steps, NKV, group, dim).transpose(1, 0, 2, 3)
    grouped = lax.all_to_all(by_head, ("y", "core"), split_axis=0, concat_axis=0, tiled=True)
    grouped = grouped.reshape(rows_dev, per_row, dim)
    table = entry_table(row_nodes, zi)
    ssum, sstat = suffix_part(queries, new_keys, new_values, suffix_keys, suffix_values, suffix_length)

    half = NZ // 2
    arrives = [0] + [min(off, NZ - off) for off in range(1, NZ)]
    calls = [[off for off in range(NZ) if arrives[off] in steps] for steps in CALLS]
    groups = [[calls[c] for c in cut] for cut in CUTS]
    groups[-1] = groups[-1] + [[half]]

    def attend(c):
        return node_part(q_slots, calls[c], [held[off] for off in calls[c]])

    def send_back(c):
        blocks = [outs[i] for i in CUTS[c]]
        blocks = blocks[0] if len(blocks) == 1 else jnp.concatenate(blocks, axis=1)
        return lax.all_to_all(blocks, "x", split_axis=0, concat_axis=0, tiled=True)

    def attend_due(s):
        for c, at in enumerate(DUE):
            if at == s:
                outs[c] = attend(c)

    held = {0: own}
    outs = {}
    going_up = going_down = own
    for s in range(1, half):
        going_up, going_down = lax.ppermute(going_up, "z", up), lax.ppermute(going_down, "z", down)
        if s == 2:
            packed = pack_part(table, grouped).reshape(NX, NZ * CAP, per_row, dim)
            going_up, going_down, packed = tie((going_up, going_down, packed))
            q_slots = lax.all_to_all(packed, "x", split_axis=0, concat_axis=0, tiled=True)
        elif s == 4:
            attend_due(s)
            far = lax.ppermute(q_slots[:, half * CAP : (half + 1) * CAP], "z", [(i, (i + 2) % NZ) for i in range(NZ)])
            going_up, going_down, outs, far, q_slots = tie((going_up, going_down, outs, far, q_slots))
        elif s == 5 or s == 6:
            attend_due(s)
            if s == 6:
                back = [send_back(0)]
            going_up, going_down, outs = tie((going_up, going_down, outs))
        elif s == 7:
            attend_due(s)
            far = node_part(far, [0], [held[half - 2]])
            far = lax.ppermute(far, "z", [(i, (i - 2) % NZ) for i in range(NZ)])
            going_up, going_down, outs, far, back = tie((going_up, going_down, outs, far, back))
        held[NZ - s], held[s] = going_up, going_down
    attend_due(half)
    last = jnp.concatenate([outs[c] for c in CUTS[1]] + [far], axis=1)
    back.append(lax.all_to_all(last, "x", split_axis=0, concat_axis=0, tiled=True))
    merged = merge_part(table, back, groups, rows_dev, per_row)
    home = lax.all_to_all(merged, ("y", "core"), split_axis=0, concat_axis=0, tiled=True)
    return final_part(home, ssum, sstat, rows_here, steps, heads, dim)


def solution(mesh):
    fine = Mesh(mesh.devices.reshape(NZ, NX, NY, NC), ("z", "x", "y", "core"))
    ctx, kv = ("z", "x"), ("y", "core")
    everything = ctx + kv
    return jax.shard_map(
        per_device,
        mesh=fine,
        in_specs=(
            P(everything), P(everything), P(everything), P(everything), P(everything), P(everything),
            P(ctx, None),
            P(ctx, None, kv, None),
            P(ctx, None, kv, None),
            P(ctx),
        ),
        out_specs=P(everything),
        check_vma=False,
    )
```

```python
import functools
import math

import jax
import jax.numpy as jnp
from jax import lax
from jax.experimental import pallas as pl
from jax.experimental.pallas import tpu as pltpu
from jax.sharding import Mesh
from jax.sharding import PartitionSpec as P

NZ, NX, NY, NC = 16, 4, 4, 2
NKV = NY * NC
CAP = 3
CALLS = [[0, 1], [2, 3, 4], [5], [6], [7]]
DUE = [4, 6, 6, 7, 8]
CUTS = [[0, 1, 2], [3, 4]]
F32 = jnp.float32
BF16 = jnp.bfloat16
VMEM_LIMIT = 20 * 1024 * 1024
VM = pl.BlockSpec(memory_space=pltpu.VMEM)


SMALL = pl.CostEstimate(flops=1 << 10, bytes_accessed=1 << 10, transcendentals=0)


def params():
    return pltpu.CompilerParams(vmem_limit_bytes=VMEM_LIMIT)


def split3(x):
    hi = x.astype(BF16).astype(F32)
    rest = x - hi
    mid = rest.astype(BF16).astype(F32)
    return [hi, mid, rest - mid]


def lane_stats(values, rows):
    lane = lax.broadcasted_iota(jnp.int32, (rows, 128), 1)
    out = jnp.zeros((rows, 128), F32)
    for i, v in enumerate(values):
        out = jnp.where(lane == i, v, out)
    return out


def pad_rows(x, rows):
    if x.shape[0] == rows:
        return x
    return jnp.concatenate([x, jnp.zeros((rows - x.shape[0], x.shape[1]), x.dtype)], axis=0)


def suffix_kernel(scale, steps, len_ref, q_ref, k_ref, nk_ref, v_ref, nv_ref, sum_ref, stat_ref):
    row = pl.program_id(0)
    length = len_ref[row]
    q = q_ref[0]
    heads = q.shape[0] // steps
    kvh = nk_ref.shape[1] // steps
    group = heads // kvh

    def scores(keys):
        return lax.dot_general(q, keys, (((1,), (1,)), ((), ())), preferred_element_type=F32) * scale

    def masks(cols):
        qi = lax.broadcasted_iota(jnp.int32, (q.shape[0], cols), 0)
        ci = lax.broadcasted_iota(jnp.int32, (q.shape[0], cols), 1)
        same = ((qi % heads) // group) == (ci % kvh)
        return same, ci // kvh, qi // heads

    same, slot, _ = masks(k_ref.shape[1])
    own = jnp.where(same & (slot < length), scores(k_ref[0]), -jnp.inf)
    same, slot, step = masks(nk_ref.shape[1])
    fresh = jnp.where(same & (slot <= step), scores(nk_ref[0]), -jnp.inf)
    top = jnp.maximum(jnp.max(own, axis=1, keepdims=True), jnp.max(fresh, axis=1, keepdims=True))
    own_w = jnp.exp(own - top)
    fresh_w = jnp.exp(fresh - top)
    total = jnp.sum(own_w, axis=1, keepdims=True) + jnp.sum(fresh_w, axis=1, keepdims=True)
    acc = jnp.dot(own_w.astype(BF16), v_ref[0], preferred_element_type=F32)
    acc = acc + jnp.dot(fresh_w.astype(BF16), nv_ref[0], preferred_element_type=F32)
    sum_ref[0] = acc
    both = lane_stats([top, total], q.shape[0])
    for b in range(0, q.shape[0], 128):
        columns = both[b : b + 128]
        stat_ref[0, :, b : b + 128] = pad_rows(columns, 128).T[:8, : columns.shape[0]]


def suffix_part(queries, new_keys, new_values, suffix_keys, suffix_values, suffix_length):
    rows, steps, heads, dim = queries.shape
    slots, kvh = suffix_keys.shape[1:3]
    qn, kn, fn = steps * heads, slots * kvh, steps * kvh
    block = lambda n: pl.BlockSpec((1, n, dim), lambda i, s: (i, 0, 0))
    ssum, sstat = pl.pallas_call(
        functools.partial(suffix_kernel, dim ** (-0.5), steps),
        grid_spec=pltpu.PrefetchScalarGridSpec(
            num_scalar_prefetch=1,
            grid=(rows,),
            in_specs=[block(qn), block(kn), block(fn), block(kn), block(fn)],
            out_specs=[block(qn), pl.BlockSpec((1, 8, qn), lambda i, s: (i, 0, 0))],
        ),
        out_shape=[
            jax.ShapeDtypeStruct((rows, qn, dim), F32),
            jax.ShapeDtypeStruct((rows, 8, qn), F32),
        ],
        compiler_params=params(),
        cost_estimate=pl.CostEstimate(
            flops=4 * rows * qn * kn * dim, bytes_accessed=4 << 20, transcendentals=rows * qn * kn
        ),
        name="suffix",
    )(
        suffix_length,
        queries.reshape(rows, qn, dim),
        suffix_keys.reshape(rows, kn, dim),
        new_keys.reshape(rows, fn, dim),
        suffix_values.reshape(rows, kn, dim),
        new_values.reshape(rows, fn, dim),
    )
    group = heads // kvh
    stat = sstat[:, :2].reshape(rows, 2, steps, kvh, group).transpose(1, 3, 0, 2, 4)
    stat = stat.reshape(2, kvh, rows, steps * group)
    return ssum, jnp.pad(stat, ((0, 0), (0, 0), (0, 0), (0, 128 - steps * group)))


def pack_kernel(table_ref, q_ref, out_ref):
    rows = q_ref.shape[0]

    def one(j, carry):
        entry = jnp.maximum(table_ref[j], 0)
        out_ref[j] = q_ref[lax.rem(entry, rows)]
        return carry

    lax.fori_loop(0, out_ref.shape[0], one, 0, unroll=8)


def pack_part(table, grouped):
    rows, per_row, dim = grouped.shape
    return pl.pallas_call(
        pack_kernel,
        grid_spec=pltpu.PrefetchScalarGridSpec(
            num_scalar_prefetch=1, grid=(), in_specs=[VM], out_specs=VM
        ),
        out_shape=jax.ShapeDtypeStruct((table.shape[0], per_row, dim), BF16),
        compiler_params=params(),
        cost_estimate=SMALL,
        name="pack",
    )(table, grouped)


def node_kernel(scale, count, *refs):
    q_refs, kv_refs, out_ref = refs[:count], refs[count:-1], refs[-1]
    stats = []
    for i in range(count):
        q = q_refs[i][...]
        each = q.shape[1] * q.shape[2]
        m_all = NX * each
        q = q.reshape(m_all, q.shape[3])
        slots = (kv_refs[i].shape[0] - 16) // 2
        keys, values, tail = kv_refs[i][:slots], kv_refs[i][slots : 2 * slots], kv_refs[i][2 * slots :]
        length = tail[:8].astype(F32)
        length = length[0:1, :] * 32.0 + length[1:2, :]
        length = jnp.concatenate([length] * (slots // 128), axis=1)
        s = lax.dot_general(q, keys, (((1,), (1,)), ((), ())), preferred_element_type=F32)
        col = lax.broadcasted_iota(jnp.int32, (1, slots), 1).astype(F32)
        s = jnp.where(col < length, s, -jnp.inf)
        top = jnp.max(s, axis=1, keepdims=True)
        w = jnp.exp2((s - top) * (scale * math.log2(math.e)))
        total = jnp.sum(w, axis=1, keepdims=True)
        o = jnp.dot(w.astype(BF16), values, preferred_element_type=F32) * (1.0 / total)
        o = o.astype(BF16).reshape(NX, each, o.shape[1])
        for x in range(NX):
            out_ref[x, i * each : (i + 1) * each] = o[x]
        stats += split3(top * scale) + split3(total)
    packed = lane_stats(stats, m_all)
    for x in range(NX):
        block = pad_rows(packed[x * each : (x + 1) * each], 128)
        out_ref[x, count * each :] = block.T[: out_ref.shape[1] - count * each].astype(BF16)


def stat_rows(count):
    return -(-6 * count // 16) * 16


def node_part(q_slots, places, kvs):
    count = len(places)
    per_row, dim = q_slots.shape[2:]
    each = CAP * per_row
    work = NX * each * 1024 * count
    shape = (NX, count * each + stat_rows(count), dim)
    q_block = lambda off: pl.BlockSpec((NX, CAP, per_row, dim), lambda i: (0, off, 0, 0))
    return pl.pallas_call(
        functools.partial(node_kernel, dim ** (-0.5), count),
        grid=(1,),
        in_specs=[q_block(p) for p in places] + [VM] * len(kvs),
        out_specs=pl.BlockSpec(shape, lambda i: (0, 0, 0)),
        out_shape=jax.ShapeDtypeStruct(shape, BF16),
        compiler_params=params(),
        cost_estimate=SMALL,
        name="node",
    )(*[q_slots] * count, *kvs)


def merge_kernel(groups, rows, per_row, table_ref, *refs):
    arrived = refs[: len(groups)]
    out_ref, e_out, e_max, e_total = refs[-4:]
    each = CAP * per_row
    for ref, steps in zip(arrived, groups):
        base = 0
        for offsets in steps:
            count = len(offsets)
            for x in range(NX):
                tile = ref[x, base + count * each : base + count * each + stat_rows(count)].astype(F32)
                for i, off in enumerate(offsets):
                    top = tile[6 * i : 6 * i + 1] + tile[6 * i + 1 : 6 * i + 2] + tile[6 * i + 2 : 6 * i + 3]
                    total = tile[6 * i + 3 : 6 * i + 4] + tile[6 * i + 4 : 6 * i + 5] + tile[6 * i + 5 : 6 * i + 6]
                    for k in range(CAP):
                        entry = table_ref[(x * NZ + off) * CAP + k]
                        entry = jnp.where(entry < 0, 2 * rows, entry)
                        start = base + i * each + k * per_row
                        e_out[entry] = ref[x, start : start + per_row]
                        if k:
                            top_k = pltpu.roll(top, 128 - k * per_row, 1)
                            total_k = pltpu.roll(total, 128 - k * per_row, 1)
                        else:
                            top_k, total_k = top, total
                        e_max[pl.ds(entry, 1), :] = top_k
                        e_total[pl.ds(entry, 1), :] = total_k
            base += count * each + stat_rows(count)
    m0, m1 = e_max[:rows], e_max[rows : 2 * rows]
    top = jnp.maximum(m0, m1)
    w0 = e_total[:rows] * jnp.exp(m0 - top)
    w1 = e_total[rows : 2 * rows] * jnp.exp(m1 - top)
    total = w0 + w1
    f0 = pad_rows(w0 / total, 128).T
    f1 = pad_rows(w1 / total, 128).T
    rows_here = rows // NKV
    pieces = split3(top) + split3(total)
    tail = rows_here * per_row
    for y in range(NKV):
        for r in range(rows_here):
            row = y * rows_here + r
            o = f0[:per_row, row : row + 1] * e_out[row].astype(F32)
            o = o + f1[:per_row, row : row + 1] * e_out[rows + row].astype(F32)
            out_ref[y, r * per_row : (r + 1) * per_row] = o.astype(BF16)
        part = [p[y * rows_here : (y + 1) * rows_here] for p in pieces]
        part = pad_rows(jnp.concatenate(part, axis=0), out_ref.shape[1] - tail)
        out_ref[y, tail:] = part.astype(BF16)


def merge_part(table, arrived, groups, rows, per_row):
    dim = arrived[0].shape[2]
    rows_here = rows // NKV
    shape = (NKV, rows_here * per_row + stat_rows(rows_here), dim)
    return pl.pallas_call(
        functools.partial(merge_kernel, groups, rows, per_row),
        grid_spec=pltpu.PrefetchScalarGridSpec(
            num_scalar_prefetch=1,
            grid=(),
            in_specs=[VM] * len(arrived),
            out_specs=VM,
            scratch_shapes=[
                pltpu.VMEM((2 * rows + 1, per_row, dim), BF16),
                pltpu.VMEM((2 * rows + 8, 128), F32),
                pltpu.VMEM((2 * rows + 8, 128), F32),
            ],
        ),
        out_shape=jax.ShapeDtypeStruct(shape, BF16),
        compiler_params=params(),
        cost_estimate=pl.CostEstimate(flops=1 << 22, bytes_accessed=4 << 20, transcendentals=1 << 16),
        name="merge",
    )(table, *arrived)


def final_kernel(rows, steps, arrived_ref, ssum_ref, sstat_ref, out_ref, res_ref):
    group = ssum_ref.shape[2]
    per_row = steps * group
    here = rows * per_row
    w_prefix, w_suffix = [], []
    for j in range(NKV):
        tile = arrived_ref[j, here:].astype(F32)
        part = [tile[i * rows : (i + 1) * rows] for i in range(6)]
        p_max, p_total = part[0] + part[1] + part[2], part[3] + part[4] + part[5]
        s_max, s_total = sstat_ref[0, j], sstat_ref[1, j]
        top = jnp.maximum(p_max, s_max)
        wp = p_total * jnp.exp(p_max - top)
        ws = jnp.exp(s_max - top)
        inverse = 1.0 / (wp + ws * s_total)
        w_prefix.append(wp * inverse)
        w_suffix.append(ws * inverse)
    w_prefix = pad_rows(jnp.concatenate(w_prefix, axis=0), 128).T
    w_suffix = pad_rows(jnp.concatenate(w_suffix, axis=0), 128).T
    for j in range(NKV):
        for r in range(rows):
            at = j * rows + r
            o = arrived_ref[j, r * per_row : (r + 1) * per_row].astype(F32)
            own = ssum_ref[r * steps : (r + 1) * steps, j].reshape(per_row, o.shape[1])
            mixed = w_prefix[:per_row, at : at + 1] * o + w_suffix[:per_row, at : at + 1] * own
            res_ref[r * steps : (r + 1) * steps, j] = mixed.reshape(steps, group, o.shape[1])
    out_ref[...] = res_ref[...].reshape(out_ref.shape).astype(BF16)


def final_part(arrived, ssum, sstat, rows, steps, heads, dim):
    shape = (rows * steps, NKV, heads // NKV, dim)
    out = pl.pallas_call(
        functools.partial(final_kernel, rows, steps),
        in_specs=[VM] * 3,
        out_specs=VM,
        out_shape=jax.ShapeDtypeStruct((rows * steps * heads, dim), BF16),
        scratch_shapes=[pltpu.VMEM(shape, F32)],
        compiler_params=params(),
        cost_estimate=pl.CostEstimate(flops=1 << 22, bytes_accessed=4 << 20, transcendentals=1 << 16),
        name="final",
    )(arrived, ssum.reshape(shape), sstat)
    return out.reshape(rows, steps, heads, dim)


def entry_table(row_nodes, zi):
    rows, depth = row_nodes.shape
    node = row_nodes.T.reshape(rows * depth)
    entry = jnp.arange(rows * depth, dtype=jnp.int32)
    earlier = (node[:, None] == node[None, :]) & (entry[None, :] < entry[:, None])
    rank = jnp.sum(earlier.astype(jnp.int32), axis=1)
    offset = jnp.mod(node // NX - zi, NZ)
    place = (jnp.mod(node, NX) * NZ + offset) * CAP + rank
    hit = place[:, None] == jnp.arange(NX * NZ * CAP, dtype=jnp.int32)[None, :]
    return jnp.sum(jnp.where(hit, entry[:, None] + 1, 0), axis=0) - 1


def per_device(
    queries, new_keys, new_values, suffix_keys, suffix_values, suffix_length,
    row_nodes, prefix_keys, prefix_values, node_length,
):
    rows_dev, depth = row_nodes.shape
    rows_here, steps, heads, dim = queries.shape
    group = heads // NKV
    per_row = steps * group
    zi = lax.axis_index("z")
    slots = prefix_keys.shape[1]
    length = node_length[0]
    digits = jnp.stack([length // 32, length % 32]).astype(BF16)
    tail = jnp.broadcast_to(jnp.pad(digits, (0, 14))[:, None], (16, dim))
    own = jnp.concatenate([prefix_keys.reshape(slots, dim), prefix_values.reshape(slots, dim), tail])
    up = [(i, (i + 1) % NZ) for i in range(NZ)]
    down = [(i, (i - 1) % NZ) for i in range(NZ)]

    tie = lax.optimization_barrier
    by_head = queries.reshape(rows_here * steps, NKV, group, dim).transpose(1, 0, 2, 3)
    grouped = lax.all_to_all(by_head, ("y", "core"), split_axis=0, concat_axis=0, tiled=True)
    grouped = grouped.reshape(rows_dev, per_row, dim)
    table = entry_table(row_nodes, zi)
    ssum, sstat = suffix_part(queries, new_keys, new_values, suffix_keys, suffix_values, suffix_length)

    half = NZ // 2
    arrives = [0] + [min(off, NZ - off) for off in range(1, NZ)]
    calls = [[off for off in range(NZ) if arrives[off] in steps] for steps in CALLS]
    groups = [[calls[c] for c in cut] for cut in CUTS]
    groups[-1] = groups[-1] + [[half]]

    def attend(c):
        return node_part(q_slots, calls[c], [held[off] for off in calls[c]])

    def send_back(c):
        blocks = [outs[i] for i in CUTS[c]]
        blocks = blocks[0] if len(blocks) == 1 else jnp.concatenate(blocks, axis=1)
        return lax.all_to_all(blocks, "x", split_axis=0, concat_axis=0, tiled=True)

    def attend_due(s):
        for c, at in enumerate(DUE):
            if at == s:
                outs[c] = attend(c)

    held = {0: own}
    outs = {}
    going_up = going_down = own
    for s in range(1, half):
        going_up, going_down = lax.ppermute(going_up, "z", up), lax.ppermute(going_down, "z", down)
        if s == 2:
            packed = pack_part(table, grouped).reshape(NX, NZ * CAP, per_row, dim)
            q_slots = lax.all_to_all(packed, "x", split_axis=0, concat_axis=0, tiled=True)
        elif s == 4:
            attend_due(s)
            far = lax.ppermute(q_slots[:, half * CAP : (half + 1) * CAP], "z", [(i, (i + 2) % NZ) for i in range(NZ)])
            going_up, going_down, outs, far, q_slots = tie((going_up, going_down, outs, far, q_slots))
        elif s == 6:
            attend_due(s)
            back = [send_back(0)]
            going_up, going_down, outs = tie((going_up, going_down, outs))
        elif s == 7:
            attend_due(s)
            far = node_part(far, [0], [held[half - 2]])
            far = lax.ppermute(far, "z", [(i, (i - 2) % NZ) for i in range(NZ)])
            going_up, going_down, outs, far, back = tie((going_up, going_down, outs, far, back))
        held[NZ - s], held[s] = going_up, going_down
    attend_due(half)
    last = jnp.concatenate([outs[c] for c in CUTS[1]] + [far], axis=1)
    back.append(lax.all_to_all(last, "x", split_axis=0, concat_axis=0, tiled=True))
    merged = merge_part(table, back, groups, rows_dev, per_row)
    home = lax.all_to_all(merged, ("y", "core"), split_axis=0, concat_axis=0, tiled=True)
    return final_part(home, ssum, sstat, rows_here, steps, heads, dim)


def solution(mesh):
    fine = Mesh(mesh.devices.reshape(NZ, NX, NY, NC), ("z", "x", "y", "core"))
    ctx, kv = ("z", "x"), ("y", "core")
    everything = ctx + kv
    return jax.shard_map(
        per_device,
        mesh=fine,
        in_specs=(
            P(everything), P(everything), P(everything), P(everything), P(everything), P(everything),
            P(ctx, None),
            P(ctx, None, kv, None),
            P(ctx, None, kv, None),
            P(ctx),
        ),
        out_specs=P(everything),
        check_vma=False,
    )
```

```python
import functools
import math

import jax
import jax.numpy as jnp
from jax import lax
from jax.experimental import pallas as pl
from jax.experimental.pallas import tpu as pltpu
from jax.sharding import Mesh
from jax.sharding import PartitionSpec as P

NZ, NX, NY, NC = 16, 4, 4, 2
NKV = NY * NC
CAP = 3
CALLS = [[0, 1], [2, 3, 4], [5], [6], [7]]
DUE = [4, 6, 6, 7, 8]
CUTS = [[0, 1, 2], [3, 4]]
F32 = jnp.float32
BF16 = jnp.bfloat16
VMEM_LIMIT = 10 * 1024 * 1024
VM = pl.BlockSpec(memory_space=pltpu.VMEM)


SMALL = pl.CostEstimate(flops=1 << 10, bytes_accessed=1 << 10, transcendentals=0)


def params():
    return pltpu.CompilerParams(vmem_limit_bytes=VMEM_LIMIT)


def split3(x):
    hi = x.astype(BF16).astype(F32)
    rest = x - hi
    mid = rest.astype(BF16).astype(F32)
    return [hi, mid, rest - mid]


def lane_stats(values, rows):
    lane = lax.broadcasted_iota(jnp.int32, (rows, 128), 1)
    out = jnp.zeros((rows, 128), F32)
    for i, v in enumerate(values):
        out = jnp.where(lane == i, v, out)
    return out


def pad_rows(x, rows):
    if x.shape[0] == rows:
        return x
    return jnp.concatenate([x, jnp.zeros((rows - x.shape[0], x.shape[1]), x.dtype)], axis=0)


def suffix_kernel(scale, steps, len_ref, q_ref, k_ref, nk_ref, v_ref, nv_ref, sum_ref, stat_ref):
    row = pl.program_id(0)
    length = len_ref[row]
    q = q_ref[0]
    heads = q.shape[0] // steps
    kvh = nk_ref.shape[1] // steps
    group = heads // kvh

    def scores(keys):
        return lax.dot_general(q, keys, (((1,), (1,)), ((), ())), preferred_element_type=F32) * scale

    def masks(cols):
        qi = lax.broadcasted_iota(jnp.int32, (q.shape[0], cols), 0)
        ci = lax.broadcasted_iota(jnp.int32, (q.shape[0], cols), 1)
        same = ((qi % heads) // group) == (ci % kvh)
        return same, ci // kvh, qi // heads

    same, slot, _ = masks(k_ref.shape[1])
    own = jnp.where(same & (slot < length), scores(k_ref[0]), -jnp.inf)
    same, slot, step = masks(nk_ref.shape[1])
    fresh = jnp.where(same & (slot <= step), scores(nk_ref[0]), -jnp.inf)
    top = jnp.maximum(jnp.max(own, axis=1, keepdims=True), jnp.max(fresh, axis=1, keepdims=True))
    own_w = jnp.exp(own - top)
    fresh_w = jnp.exp(fresh - top)
    total = jnp.sum(own_w, axis=1, keepdims=True) + jnp.sum(fresh_w, axis=1, keepdims=True)
    acc = jnp.dot(own_w.astype(BF16), v_ref[0], preferred_element_type=F32)
    acc = acc + jnp.dot(fresh_w.astype(BF16), nv_ref[0], preferred_element_type=F32)
    sum_ref[0] = acc
    both = lane_stats([top, total], q.shape[0])
    for b in range(0, q.shape[0], 128):
        columns = both[b : b + 128]
        stat_ref[0, :, b : b + 128] = pad_rows(columns, 128).T[:8, : columns.shape[0]]


def suffix_part(queries, new_keys, new_values, suffix_keys, suffix_values, suffix_length):
    rows, steps, heads, dim = queries.shape
    slots, kvh = suffix_keys.shape[1:3]
    qn, kn, fn = steps * heads, slots * kvh, steps * kvh
    block = lambda n: pl.BlockSpec((1, n, dim), lambda i, s: (i, 0, 0))
    ssum, sstat = pl.pallas_call(
        functools.partial(suffix_kernel, dim ** (-0.5), steps),
        grid_spec=pltpu.PrefetchScalarGridSpec(
            num_scalar_prefetch=1,
            grid=(rows,),
            in_specs=[block(qn), block(kn), block(fn), block(kn), block(fn)],
            out_specs=[block(qn), pl.BlockSpec((1, 8, qn), lambda i, s: (i, 0, 0))],
        ),
        out_shape=[
            jax.ShapeDtypeStruct((rows, qn, dim), F32),
            jax.ShapeDtypeStruct((rows, 8, qn), F32),
        ],
        compiler_params=params(),
        cost_estimate=pl.CostEstimate(
            flops=4 * rows * qn * kn * dim, bytes_accessed=4 << 20, transcendentals=rows * qn * kn
        ),
        name="suffix",
    )(
        suffix_length,
        queries.reshape(rows, qn, dim),
        suffix_keys.reshape(rows, kn, dim),
        new_keys.reshape(rows, fn, dim),
        suffix_values.reshape(rows, kn, dim),
        new_values.reshape(rows, fn, dim),
    )
    group = heads // kvh
    stat = sstat[:, :2].reshape(rows, 2, steps, kvh, group).transpose(1, 3, 0, 2, 4)
    stat = stat.reshape(2, kvh, rows, steps * group)
    return ssum, jnp.pad(stat, ((0, 0), (0, 0), (0, 0), (0, 128 - steps * group)))


def pack_kernel(table_ref, q_ref, out_ref):
    rows = q_ref.shape[0]

    def one(j, carry):
        entry = jnp.maximum(table_ref[j], 0)
        out_ref[j] = q_ref[lax.rem(entry, rows)]
        return carry

    lax.fori_loop(0, out_ref.shape[0], one, 0, unroll=8)


def pack_part(table, grouped):
    rows, per_row, dim = grouped.shape
    return pl.pallas_call(
        pack_kernel,
        grid_spec=pltpu.PrefetchScalarGridSpec(
            num_scalar_prefetch=1, grid=(), in_specs=[VM], out_specs=VM
        ),
        out_shape=jax.ShapeDtypeStruct((table.shape[0], per_row, dim), BF16),
        compiler_params=params(),
        cost_estimate=SMALL,
        name="pack",
    )(table, grouped)


def node_kernel(scale, count, *refs):
    q_refs, kv_refs, out_ref = refs[:count], refs[count:-1], refs[-1]
    stats = []
    for i in range(count):
        q = q_refs[i][...]
        each = q.shape[1] * q.shape[2]
        m_all = NX * each
        q = q.reshape(m_all, q.shape[3])
        slots = (kv_refs[i].shape[0] - 16) // 2
        keys, values, tail = kv_refs[i][:slots], kv_refs[i][slots : 2 * slots], kv_refs[i][2 * slots :]
        length = tail[:8].astype(F32)
        length = length[0:1, :] * 32.0 + length[1:2, :]
        length = jnp.concatenate([length] * (slots // 128), axis=1)
        s = lax.dot_general(q, keys, (((1,), (1,)), ((), ())), preferred_element_type=F32)
        col = lax.broadcasted_iota(jnp.int32, (1, slots), 1).astype(F32)
        s = jnp.where(col < length, s, -jnp.inf)
        top = jnp.max(s, axis=1, keepdims=True)
        w = jnp.exp2((s - top) * (scale * math.log2(math.e)))
        total = jnp.sum(w, axis=1, keepdims=True)
        o = jnp.dot(w.astype(BF16), values, preferred_element_type=F32) * (1.0 / total)
        o = o.astype(BF16).reshape(NX, each, o.shape[1])
        for x in range(NX):
            out_ref[x, i * each : (i + 1) * each] = o[x]
        stats += split3(top * scale) + split3(total)
    packed = lane_stats(stats, m_all)
    for x in range(NX):
        block = pad_rows(packed[x * each : (x + 1) * each], 128)
        out_ref[x, count * each :] = block.T[: out_ref.shape[1] - count * each].astype(BF16)


def stat_rows(count):
    return -(-6 * count // 16) * 16


def node_part(q_slots, places, kvs):
    count = len(places)
    per_row, dim = q_slots.shape[2:]
    each = CAP * per_row
    work = NX * each * 1024 * count
    shape = (NX, count * each + stat_rows(count), dim)
    q_block = lambda off: pl.BlockSpec((NX, CAP, per_row, dim), lambda i: (0, off, 0, 0))
    return pl.pallas_call(
        functools.partial(node_kernel, dim ** (-0.5), count),
        grid=(1,),
        in_specs=[q_block(p) for p in places] + [VM] * len(kvs),
        out_specs=pl.BlockSpec(shape, lambda i: (0, 0, 0)),
        out_shape=jax.ShapeDtypeStruct(shape, BF16),
        compiler_params=params(),
        cost_estimate=SMALL,
        name="node",
    )(*[q_slots] * count, *kvs)


def merge_kernel(groups, rows, per_row, table_ref, *refs):
    arrived = refs[: len(groups)]
    out_ref, e_out, e_max, e_total = refs[-4:]
    each = CAP * per_row
    for ref, steps in zip(arrived, groups):
        base = 0
        for offsets in steps:
            count = len(offsets)
            for x in range(NX):
                tile = ref[x, base + count * each : base + count * each + stat_rows(count)].astype(F32)
                for i, off in enumerate(offsets):
                    top = tile[6 * i : 6 * i + 1] + tile[6 * i + 1 : 6 * i + 2] + tile[6 * i + 2 : 6 * i + 3]
                    total = tile[6 * i + 3 : 6 * i + 4] + tile[6 * i + 4 : 6 * i + 5] + tile[6 * i + 5 : 6 * i + 6]
                    for k in range(CAP):
                        entry = table_ref[(x * NZ + off) * CAP + k]
                        entry = jnp.where(entry < 0, 2 * rows, entry)
                        start = base + i * each + k * per_row
                        e_out[entry] = ref[x, start : start + per_row]
                        if k:
                            top_k = pltpu.roll(top, 128 - k * per_row, 1)
                            total_k = pltpu.roll(total, 128 - k * per_row, 1)
                        else:
                            top_k, total_k = top, total
                        e_max[pl.ds(entry, 1), :] = top_k
                        e_total[pl.ds(entry, 1), :] = total_k
            base += count * each + stat_rows(count)
    m0, m1 = e_max[:rows], e_max[rows : 2 * rows]
    top = jnp.maximum(m0, m1)
    w0 = e_total[:rows] * jnp.exp(m0 - top)
    w1 = e_total[rows : 2 * rows] * jnp.exp(m1 - top)
    total = w0 + w1
    f0 = pad_rows(w0 / total, 128).T
    f1 = pad_rows(w1 / total, 128).T
    rows_here = rows // NKV
    pieces = split3(top) + split3(total)
    tail = rows_here * per_row
    for y in range(NKV):
        for r in range(rows_here):
            row = y * rows_here + r
            o = f0[:per_row, row : row + 1] * e_out[row].astype(F32)
            o = o + f1[:per_row, row : row + 1] * e_out[rows + row].astype(F32)
            out_ref[y, r * per_row : (r + 1) * per_row] = o.astype(BF16)
        part = [p[y * rows_here : (y + 1) * rows_here] for p in pieces]
        part = pad_rows(jnp.concatenate(part, axis=0), out_ref.shape[1] - tail)
        out_ref[y, tail:] = part.astype(BF16)


def merge_part(table, arrived, groups, rows, per_row):
    dim = arrived[0].shape[2]
    rows_here = rows // NKV
    shape = (NKV, rows_here * per_row + stat_rows(rows_here), dim)
    return pl.pallas_call(
        functools.partial(merge_kernel, groups, rows, per_row),
        grid_spec=pltpu.PrefetchScalarGridSpec(
            num_scalar_prefetch=1,
            grid=(),
            in_specs=[VM] * len(arrived),
            out_specs=VM,
            scratch_shapes=[
                pltpu.VMEM((2 * rows + 1, per_row, dim), BF16),
                pltpu.VMEM((2 * rows + 8, 128), F32),
                pltpu.VMEM((2 * rows + 8, 128), F32),
            ],
        ),
        out_shape=jax.ShapeDtypeStruct(shape, BF16),
        compiler_params=params(),
        cost_estimate=pl.CostEstimate(flops=1 << 22, bytes_accessed=4 << 20, transcendentals=1 << 16),
        name="merge",
    )(table, *arrived)


def final_kernel(rows, steps, arrived_ref, ssum_ref, sstat_ref, out_ref, res_ref):
    group = ssum_ref.shape[2]
    per_row = steps * group
    here = rows * per_row
    w_prefix, w_suffix = [], []
    for j in range(NKV):
        tile = arrived_ref[j, here:].astype(F32)
        part = [tile[i * rows : (i + 1) * rows] for i in range(6)]
        p_max, p_total = part[0] + part[1] + part[2], part[3] + part[4] + part[5]
        s_max, s_total = sstat_ref[0, j], sstat_ref[1, j]
        top = jnp.maximum(p_max, s_max)
        wp = p_total * jnp.exp(p_max - top)
        ws = jnp.exp(s_max - top)
        inverse = 1.0 / (wp + ws * s_total)
        w_prefix.append(wp * inverse)
        w_suffix.append(ws * inverse)
    w_prefix = pad_rows(jnp.concatenate(w_prefix, axis=0), 128).T
    w_suffix = pad_rows(jnp.concatenate(w_suffix, axis=0), 128).T
    for j in range(NKV):
        for r in range(rows):
            at = j * rows + r
            o = arrived_ref[j, r * per_row : (r + 1) * per_row].astype(F32)
            own = ssum_ref[r * steps : (r + 1) * steps, j].reshape(per_row, o.shape[1])
            mixed = w_prefix[:per_row, at : at + 1] * o + w_suffix[:per_row, at : at + 1] * own
            res_ref[r * steps : (r + 1) * steps, j] = mixed.reshape(steps, group, o.shape[1])
    out_ref[...] = res_ref[...].reshape(out_ref.shape).astype(BF16)


def final_part(arrived, ssum, sstat, rows, steps, heads, dim):
    shape = (rows * steps, NKV, heads // NKV, dim)
    out = pl.pallas_call(
        functools.partial(final_kernel, rows, steps),
        in_specs=[VM] * 3,
        out_specs=VM,
        out_shape=jax.ShapeDtypeStruct((rows * steps * heads, dim), BF16),
        scratch_shapes=[pltpu.VMEM(shape, F32)],
        compiler_params=params(),
        cost_estimate=pl.CostEstimate(flops=1 << 22, bytes_accessed=4 << 20, transcendentals=1 << 16),
        name="final",
    )(arrived, ssum.reshape(shape), sstat)
    return out.reshape(rows, steps, heads, dim)


def entry_table(row_nodes, zi):
    rows, depth = row_nodes.shape
    node = row_nodes.T.reshape(rows * depth)
    entry = jnp.arange(rows * depth, dtype=jnp.int32)
    earlier = (node[:, None] == node[None, :]) & (entry[None, :] < entry[:, None])
    rank = jnp.sum(earlier.astype(jnp.int32), axis=1)
    offset = jnp.mod(node // NX - zi, NZ)
    place = (jnp.mod(node, NX) * NZ + offset) * CAP + rank
    hit = place[:, None] == jnp.arange(NX * NZ * CAP, dtype=jnp.int32)[None, :]
    return jnp.sum(jnp.where(hit, entry[:, None] + 1, 0), axis=0) - 1


def per_device(
    queries, new_keys, new_values, suffix_keys, suffix_values, suffix_length,
    row_nodes, prefix_keys, prefix_values, node_length,
):
    rows_dev, depth = row_nodes.shape
    rows_here, steps, heads, dim = queries.shape
    group = heads // NKV
    per_row = steps * group
    zi = lax.axis_index("z")
    slots = prefix_keys.shape[1]
    length = node_length[0]
    digits = jnp.stack([length // 32, length % 32]).astype(BF16)
    tail = jnp.broadcast_to(jnp.pad(digits, (0, 14))[:, None], (16, dim))
    own = jnp.concatenate([prefix_keys.reshape(slots, dim), prefix_values.reshape(slots, dim), tail])
    up = [(i, (i + 1) % NZ) for i in range(NZ)]
    down = [(i, (i - 1) % NZ) for i in range(NZ)]

    tie = lax.optimization_barrier
    by_head = queries.reshape(rows_here * steps, NKV, group, dim).transpose(1, 0, 2, 3)
    grouped = lax.all_to_all(by_head, ("y", "core"), split_axis=0, concat_axis=0, tiled=True)
    grouped = grouped.reshape(rows_dev, per_row, dim)
    table = entry_table(row_nodes, zi)
    ssum, sstat = suffix_part(queries, new_keys, new_values, suffix_keys, suffix_values, suffix_length)

    half = NZ // 2
    arrives = [0] + [min(off, NZ - off) for off in range(1, NZ)]
    calls = [[off for off in range(NZ) if arrives[off] in steps] for steps in CALLS]
    groups = [[calls[c] for c in cut] for cut in CUTS]
    groups[-1] = groups[-1] + [[half]]

    def attend(c):
        return node_part(q_slots, calls[c], [held[off] for off in calls[c]])

    def send_back(c):
        blocks = [outs[i] for i in CUTS[c]]
        blocks = blocks[0] if len(blocks) == 1 else jnp.concatenate(blocks, axis=1)
        return lax.all_to_all(blocks, "x", split_axis=0, concat_axis=0, tiled=True)

    def attend_due(s):
        for c, at in enumerate(DUE):
            if at == s:
                outs[c] = attend(c)

    held = {0: own}
    outs = {}
    going_up = going_down = own
    for s in range(1, half):
        going_up, going_down = lax.ppermute(going_up, "z", up), lax.ppermute(going_down, "z", down)
        if s == 2:
            packed = pack_part(table, grouped).reshape(NX, NZ * CAP, per_row, dim)
            q_slots = lax.all_to_all(packed, "x", split_axis=0, concat_axis=0, tiled=True)
        elif s == 4:
            attend_due(s)
            far = lax.ppermute(q_slots[:, half * CAP : (half + 1) * CAP], "z", [(i, (i + 2) % NZ) for i in range(NZ)])
            going_up, going_down, outs, far, q_slots = tie((going_up, going_down, outs, far, q_slots))
        elif s == 6:
            attend_due(s)
            back = [send_back(0)]
            going_up, going_down, outs = tie((going_up, going_down, outs))
        elif s == 7:
            attend_due(s)
            far = node_part(far, [0], [held[half - 2]])
            far = lax.ppermute(far, "z", [(i, (i - 2) % NZ) for i in range(NZ)])
            going_up, going_down, outs, far, back = tie((going_up, going_down, outs, far, back))
        held[NZ - s], held[s] = going_up, going_down
    attend_due(half)
    last = jnp.concatenate([outs[c] for c in CUTS[1]] + [far], axis=1)
    back.append(lax.all_to_all(last, "x", split_axis=0, concat_axis=0, tiled=True))
    merged = merge_part(table, back, groups, rows_dev, per_row)
    home = lax.all_to_all(merged, ("y", "core"), split_axis=0, concat_axis=0, tiled=True)
    return final_part(home, ssum, sstat, rows_here, steps, heads, dim)


def solution(mesh):
    fine = Mesh(mesh.devices.reshape(NZ, NX, NY, NC), ("z", "x", "y", "core"))
    ctx, kv = ("z", "x"), ("y", "core")
    everything = ctx + kv
    return jax.shard_map(
        per_device,
        mesh=fine,
        in_specs=(
            P(everything), P(everything), P(everything), P(everything), P(everything), P(everything),
            P(ctx, None),
            P(ctx, None, kv, None),
            P(ctx, None, kv, None),
            P(ctx),
        ),
        out_specs=P(everything),
        check_vma=False,
    )
```
